256 devices in a mesh: clip: 4 (over y), blk: 16 (over z_lo, x, core), head: 4 (over z_hi).
Axes of the slice: x: 4, y: 4, z: 8 (z_hi: 4, z_lo: 2; z = z_hi * 2 + z_lo), core: 2. Of those that a mesh axis runs over, the one named last changes fastest.
Arguments:
- query_rows: bfloat16 [16384, 2560], P(('clip', 'blk', 'head')), parts along dimension 0, may hold values from -32 to 32
- key_rows: bfloat16 [16384, 2560], P(('clip', 'blk', 'head')), parts along dimension 0, may hold values from -12 to 12
- value_rows: bfloat16 [16384, 2560], P(('clip', 'blk', 'head')), parts along dimension 0, may hold values from -12 to 12
- query_tan: bfloat16 [16384, 2560], P(('clip', 'blk', 'head')), parts along dimension 0, may hold values from -6 to 6
- key_tan: bfloat16 [16384, 2560], P(('clip', 'blk', 'head')), parts along dimension 0, may hold values from -6 to 6
- value_tan: bfloat16 [16384, 2560], P(('clip', 'blk', 'head')), parts along dimension 0, may hold values from -6 to 6
Outputs:
- attended: bfloat16 [16384, 2560], P(('clip', 'blk', 'head')), parts along dimension 0
- attended_tan: bfloat16 [16384, 2560], P(('clip', 'blk', 'head')), parts along dimension 0
The draws below stay inside these ranges and needn't reach their ends.
There are 4 independent parts, one for each index of `clip`. The reference program is written for one: setup_inputs(seed, part) draws one part's arguments, and reference() takes and returns one part's arrays. A program takes and returns all parts, laid end to end along the dimension named above; each array names one. Nothing has to cross between parts.
All inputs are finite; a program needn't handle non-finite values.
Results may differ from the reference program's by a relative error of at most 0.0066.
Values may be sent and summed in bfloat16 or wider, within the bound.
No kernel may reach another device: no remote copies, remote signals or barrier semaphores. Data moves between devices by JAX's collectives and lax.ppermute only.
A program may use at most 128 MiB of HBM per device.

```python
import jax
import jax.numpy as jnp
from jax import lax

HEADS = 20
HEAD_DIM = 128
SEQ = 4096
FEAT = 2560


def draw_query_rows(key, part):
    key = jax.random.fold_in(key, 11)
    values = 1.4 * jax.random.truncated_normal(key, -6.0, 6.0, (SEQ, FEAT), jnp.float32)
    return values.astype(jnp.bfloat16)


def draw_key_rows(key, part):
    key = jax.random.fold_in(key, 12)
    values = 1.4 * jax.random.truncated_normal(key, -6.0, 6.0, (SEQ, FEAT), jnp.float32)
    return values.astype(jnp.bfloat16)


def shard_levels(own_key, extent, cuts, smallest, top_value):
    def one(dim, shards_of):
        draws = jax.random.uniform(jax.random.fold_in(jax.random.fold_in(own_key, 6), dim), (shards_of,), jnp.float32, smallest / len(cuts), top_value / len(cuts))
        return jnp.repeat(jnp.exp(draws), extent[dim] // shards_of).reshape((-1,) + (1,) * (len(extent) - dim - 1))

    factor_of = one(*cuts[0])
    for cut in cuts[1:]:
        factor_of = factor_of * one(*cut)
    return factor_of


def bell_draw(rng, dims, deviation, most, cuts=(), held_as=jnp.bfloat16):
    values = deviation * jax.random.normal(rng, dims, jnp.float32)
    if cuts:
        values = values * shard_levels(rng, dims, cuts, -0.22, 0.18)
    return jnp.clip(values, -most, most).astype(held_as)


def setup_inputs(seed: int = 0, part: int = 0) -> dict:
    key_list = jax.random.split(jax.random.key(seed), 7)
    own_keys = jax.random.split(jax.random.fold_in(key_list[6], part), 7)
    query_rows = draw_query_rows(jax.random.fold_in(jax.random.fold_in(key_list[6], part), 71), part)
    key_rows = draw_key_rows(jax.random.fold_in(jax.random.fold_in(key_list[6], part), 71), part)
    value_rows = bell_draw(own_keys[2], (SEQ, FEAT), 2.0, 12.0, ((0, 64),))
    query_tan = bell_draw(own_keys[3], (SEQ, FEAT), 1.0, 6.0, ((0, 64),))
    key_tan = bell_draw(own_keys[4], (SEQ, FEAT), 1.0, 6.0, ((0, 64),))
    value_tan = bell_draw(own_keys[5], (SEQ, FEAT), 1.0, 6.0, ((0, 64),))
    return dict(query_rows=query_rows, key_rows=key_rows, value_rows=value_rows, query_tan=query_tan, key_tan=key_tan, value_tan=value_tan)


def one_head(parts):
    query_head, key_head, value_head, querytan_head, keytan_head, valuetan_head = parts
    score_scale = HEAD_DIM ** -0.5
    scores = jnp.dot(query_head, key_head.T, preferred_element_type=jnp.float32) * score_scale
    score_tan = (jnp.dot(querytan_head, key_head.T, preferred_element_type=jnp.float32)
                 + jnp.dot(query_head, keytan_head.T, preferred_element_type=jnp.float32)) * score_scale
    row_peak = jnp.max(scores, axis=1, keepdims=True)
    weights = jnp.exp(scores - row_peak)
    row_total = jnp.sum(weights, axis=1, keepdims=True)
    tilted = weights * score_tan
    row_slope = jnp.sum(tilted, axis=1, keepdims=True)
    weights_low = weights.astype(jnp.bfloat16)
    tilted_low = tilted.astype(jnp.bfloat16)
    mixed_sum = jnp.dot(weights_low, value_head, preferred_element_type=jnp.float32)
    carried = (jnp.dot(tilted_low, value_head, preferred_element_type=jnp.float32)
               + jnp.dot(weights_low, valuetan_head, preferred_element_type=jnp.float32))
    attended = (mixed_sum / row_total).astype(jnp.bfloat16)
    attended_tan = ((carried - mixed_sum * (row_slope / row_total)) / row_total).astype(jnp.bfloat16)
    return attended, attended_tan


def by_head(array):
    return array.reshape(SEQ, HEADS, HEAD_DIM).transpose(1, 0, 2)


def by_token(array):
    return array.transpose(1, 0, 2).reshape(SEQ, FEAT)


def reference(query_rows, key_rows, value_rows, query_tan, key_tan, value_tan):
    inputs = tuple(by_head(array) for array in (query_rows, key_rows, value_rows, query_tan, key_tan, value_tan))
    attended, attended_tan = lax.map(one_head, inputs)
    return by_token(attended), by_token(attended_tan)
```

```python
import functools

import jax
import jax.numpy as jnp
from jax import lax
from jax.experimental import pallas as pl
from jax.experimental.pallas import tpu as pltpu
from jax.sharding import Mesh
from jax.sharding import PartitionSpec as P

HEAD_DIM = 128
HEADS_HERE = 5
GROUPS = 4
ROWS = 64
AXES = ("clip", "zlo", "x", "core", "zhi")
Z = ("zlo", "zhi")
SCALE = HEAD_DIM**-0.5
LOG2E = 1.4426950408889634
CHUNKS = ((0, 2), (2, 5))
VMEM = 40 * 1024 * 1024


def z_index(z):
    return (z % 2) * 4 + z // 2


def z_perm(even, odd):
    return [(z_index(z), z_index((z + (odd if z % 2 else even)) % 8)) for z in range(8)]


TO = (z_perm(-1, 1), z_perm(2, -2), z_perm(-3, 3))
BACK = (z_perm(-1, 1), z_perm(-2, 2), z_perm(-3, 3))
PAIR = z_perm(1, -1)
SWAP = [(0, 1), (1, 0)]
RIGHT = [(i, (i + 1) % 4) for i in range(4)]
LEFT = [(i, (i + 3) % 4) for i in range(4)]


def spec(shape, index_map=None):
    return pl.BlockSpec(shape, index_map) if index_map else pl.BlockSpec(memory_space=pltpu.VMEM)


def pack_body(offs, q, k, v, dq, dk, dv, *outs):
    at = 0
    for source, group in (((k, v, dk, dv), CHUNKS), ((q, dq), CHUNKS)):
        for low, high in group:
            for slot in range(4):
                out = outs[at]
                at += 1
                for a, ref in enumerate(source):
                    for h in range(low, high):
                        col = pl.multiple_of(offs[slot] + h * HEAD_DIM, HEAD_DIM)
                        out[h - low, a] = ref[:, pl.ds(col, HEAD_DIM)]


def pack(offs, arrays):
    shapes = [
        jax.ShapeDtypeStruct((high - low, count, ROWS, HEAD_DIM), jnp.bfloat16)
        for count in (4, 2)
        for low, high in CHUNKS
        for _ in range(4)
    ]
    n = len(CHUNKS)
    outs = pl.pallas_call(
        pack_body,
        out_shape=shapes,
        in_specs=[pl.BlockSpec(memory_space=pltpu.SMEM)] + [spec(None)] * 6,
        out_specs=[spec(None)] * len(shapes),
        compiler_params=pltpu.CompilerParams(vmem_limit_bytes=VMEM),
        name="pack",
    )(offs, *arrays)
    groups = [outs[4 * i : 4 * i + 4] for i in range(2 * n)]
    return groups[:n], groups[n:]


def unpack_body(offs, *refs):
    out, out_tan = refs[-2:]
    at = 0
    for low, high in CHUNKS:
        for slot in range(4):
            ref = refs[at]
            at += 1
            for h in range(low, high):
                col = pl.multiple_of(offs[slot] + h * HEAD_DIM, HEAD_DIM)
                out[:, pl.ds(col, HEAD_DIM)] = ref[h - low, 0]
                out_tan[:, pl.ds(col, HEAD_DIM)] = ref[h - low, 1]


def unpack(offs, pieces):
    shape = jax.ShapeDtypeStruct((ROWS, GROUPS * HEADS_HERE * HEAD_DIM), jnp.bfloat16)
    return pl.pallas_call(
        unpack_body,
        out_shape=[shape, shape],
        in_specs=[pl.BlockSpec(memory_space=pltpu.SMEM)] + [spec(None)] * len(pieces),
        out_specs=[spec(None)] * 2,
        compiler_params=pltpu.CompilerParams(vmem_limit_bytes=VMEM),
        name="unpack",
    )(offs, *pieces)


def fold(block):
    return block.reshape(block.shape[0] * block.shape[1], block.shape[2])


def core_part(q_ref, kv_refs, kk, vv):
    row = 0
    for ref in kv_refs:
        rows = pl.ds(row, ref.shape[0] * ROWS)
        row += ref.shape[0] * ROWS
        kk[rows, :HEAD_DIM] = fold(ref[:, 0, 0])
        kk[rows, HEAD_DIM:] = fold(ref[:, 0, 2])
        vv[rows, :HEAD_DIM] = fold(ref[:, 0, 1])
        vv[rows, HEAD_DIM:] = fold(ref[:, 0, 3])
    q, dq = fold(q_ref[:, 0, 0]), fold(q_ref[:, 0, 1])
    nt = (((1,), (1,)), ((), ()))
    dot = functools.partial(lax.dot_general, preferred_element_type=jnp.float32)
    s = dot(q, kk[:, :HEAD_DIM], nt)
    st = dot(jnp.concatenate([dq, q], axis=1), kk[...], nt)
    m = jnp.max(s, axis=1, keepdims=True)
    p = jnp.exp2((s - m) * (SCALE * LOG2E))
    t = p * st
    total = jnp.sum(p, axis=1, keepdims=True)
    slope = jnp.sum(t, axis=1, keepdims=True)
    nn = (((1,), (0,)), ((), ()))
    pv = dot(p.astype(jnp.bfloat16), vv[...], nn)
    tv = dot(t.astype(jnp.bfloat16), vv[:, :HEAD_DIM], nn)
    inverse = 1.0 / total
    att = pv[:, :HEAD_DIM] * inverse
    slope = slope * (inverse * SCALE)
    tan = (pv[:, HEAD_DIM:] + tv * SCALE) * inverse - att * slope
    return att, tan, m * SCALE + jnp.log(total), slope


def three(value):
    high = value.astype(jnp.bfloat16).astype(jnp.float32)
    rest = value - high
    middle = rest.astype(jnp.bfloat16).astype(jnp.float32)
    return high, middle, rest - middle


def far_body(count, *refs):
    q_ref, kv_refs, out, kk, vv = refs[0], refs[1 : 1 + count], *refs[1 + count :]
    att, tan, lse, slope = core_part(q_ref, kv_refs, kk, vv)
    n = att.shape[0]
    out[0, :n] = att.astype(jnp.bfloat16)
    out[0, n : 2 * n] = tan.astype(jnp.bfloat16)
    lane = lax.broadcasted_iota(jnp.int32, (n, HEAD_DIM), 1)
    stats = jnp.zeros((n, HEAD_DIM), jnp.float32)
    for i, column in enumerate(three(lse) + three(slope)):
        stats = jnp.where(lane == i, column, stats)
    flat = jnp.transpose(stats)[:16].astype(jnp.bfloat16)
    out[0, 2 * n : 2 * n + 16] = flat[:, :HEAD_DIM]
    out[0, 2 * n + 16 :] = flat[:, HEAD_DIM:]


def near_body(count, *refs):
    q_ref, kv_refs, got = refs[0], refs[1 : 1 + count], refs[1 + count]
    outs, (kk, vv) = refs[2 + count : 6 + count], refs[6 + count :]
    att, tan, lse, slope = core_part(q_ref, kv_refs, kk, vv)
    n = att.shape[0]
    att2 = got[0, :n].astype(jnp.float32)
    tan2 = got[0, n : 2 * n].astype(jnp.float32)
    flat = jnp.concatenate([got[0, 2 * n : 2 * n + 16], got[0, 2 * n + 16 :]], axis=1)
    flat = flat.astype(jnp.float32)

    def column(i):
        line = flat[i : i + 1] + flat[i + 1 : i + 2] + flat[i + 2 : i + 3]
        return jnp.transpose(jnp.broadcast_to(line, (HEAD_DIM, n)))

    lse2, slope2 = column(0), column(3)
    w1 = 1.0 / (1.0 + jnp.exp(lse2 - lse))
    w2 = 1.0 / (1.0 + jnp.exp(lse - lse2))
    tan = w1 * tan + w2 * tan2 + (w1 * w2) * (slope - slope2) * (att - att2)
    att = w1 * att + w2 * att2
    for slot in range(4):
        rows = slice(slot * ROWS, (slot + 1) * ROWS)
        outs[slot][0, 0] = att[rows].astype(jnp.bfloat16)
        outs[slot][0, 1] = tan[rows].astype(jnp.bfloat16)


def attend(q, pieces, low, high, got=None):
    heads = high - low
    keys = sum(array.shape[0] for array, _ in pieces) * ROWS
    rows = 4 * ROWS
    in_specs = [pl.BlockSpec((4, 1, 2, ROWS, HEAD_DIM), lambda h: (0, h, 0, 0, 0))]
    for array, first in pieces:
        in_specs.append(
            pl.BlockSpec(
                (array.shape[0], 1, 4, ROWS, HEAD_DIM),
                lambda h, shift=low - first: (0, h + shift, 0, 0, 0),
            )
        )
    args = [q] + [array for array, _ in pieces]
    wide = 2 * rows + 32
    if got is None:
        body = functools.partial(far_body, len(pieces))
        out_shape = jax.ShapeDtypeStruct((heads, wide, HEAD_DIM), jnp.bfloat16)
        out_specs = pl.BlockSpec((1, wide, HEAD_DIM), lambda h: (h, 0, 0))
    else:
        body = functools.partial(near_body, len(pieces))
        args.append(got)
        in_specs.append(pl.BlockSpec((1, wide, HEAD_DIM), lambda h: (h, 0, 0)))
        out_shape = [jax.ShapeDtypeStruct((heads, 2, ROWS, HEAD_DIM), jnp.bfloat16)] * 4
        out_specs = [pl.BlockSpec((1, 2, ROWS, HEAD_DIM), lambda h: (h, 0, 0, 0))] * 4
    return pl.pallas_call(
        body,
        grid=(heads,),
        out_shape=out_shape,
        in_specs=in_specs,
        out_specs=out_specs,
        scratch_shapes=[pltpu.VMEM((keys, 2 * HEAD_DIM), jnp.bfloat16)] * 2,
        compiler_params=pltpu.CompilerParams(vmem_limit_bytes=VMEM),
        cost_estimate=pl.CostEstimate(
            flops=16 * heads * rows * keys * HEAD_DIM,
            bytes_accessed=heads * keys * 4 * HEAD_DIM * 2,
            transcendentals=heads * rows * keys,
        ),
        name="far_rows" if got is None else "near_rows",
    )(*args)


def over_x(array):
    half = array.shape[0] // 2
    right = lax.ppermute(array, "x", RIGHT)
    left = lax.ppermute(array, "x", LEFT)
    if half == 0:
        return [array, right, left, lax.ppermute(right, "x", RIGHT)]
    return [
        array,
        right,
        left,
        lax.ppermute(right[:half], "x", RIGHT),
        lax.ppermute(left[half:], "x", LEFT),
    ]


def both_cores(arrays):
    return list(arrays) + [lax.ppermute(array, "core", SWAP) for array in arrays]


def per_device(query_rows, key_rows, value_rows, query_tan, key_tan, value_tan):
    group, parity = lax.axis_index("zhi"), lax.axis_index("zlo")
    step = 2 * parity - 1
    slots = jnp.stack([group, group + step, group - step, group + 2]) % GROUPS
    offs = (slots * (HEADS_HERE * HEAD_DIM)).astype(jnp.int32)
    kv, qs = pack(offs, (query_rows, key_rows, value_rows, query_tan, key_tan, value_tan))

    def spread(blocks):
        return [blocks[0]] + [lax.ppermute(b, Z, perm) for b, perm in zip(blocks[1:], TO)]

    kv = [spread(blocks) for blocks in kv]
    pieces = [
        [(array, low) for array in both_cores(over_x(jnp.stack(kv[c])))]
        for c, (low, high) in enumerate(CHUNKS)
    ]
    qs = [jnp.stack(spread(blocks)) for blocks in qs]
    far_qs = [lax.ppermute(q, Z, PAIR) for q in qs]
    back = []
    for c, (low, high) in enumerate(CHUNKS):
        sent = attend(far_qs[c], pieces[c], low, high)
        got = lax.ppermute(sent, Z, PAIR)
        outs = attend(qs[c], pieces[c], low, high, got)
        back += [outs[0]] + [lax.ppermute(o, Z, perm) for o, perm in zip(outs[1:], BACK)]
    return tuple(unpack(offs, back))


def solution(mesh):
    fine = Mesh(mesh.devices.reshape(4, 2, 4, 2, 4), AXES)
    rows = P(AXES, None)
    return jax.shard_map(
        per_device,
        mesh=fine,
        in_specs=(rows,) * 6,
        out_specs=(rows, rows),
        check_vma=False,
    )
```

```python
import functools

import jax
import jax.numpy as jnp
from jax import lax
from jax.experimental import pallas as pl
from jax.experimental.pallas import tpu as pltpu
from jax.sharding import Mesh
from jax.sharding import PartitionSpec as P

HEAD_DIM = 128
HEADS_HERE = 5
GROUPS = 4
ROWS = 64
KV_BLOCKS, Q_BLOCKS = 4 * HEADS_HERE, 2 * HEADS_HERE
AXES = ("clip", "zlo", "x", "core", "zhi")
Z = ("zlo", "zhi")
SCALE = HEAD_DIM**-0.5
LOG2E = 1.4426950408889634
CHUNKS = ((0, 2), (2, 5))
VMEM = 40 * 1024 * 1024
ORDER = (("far", 0), ("far", 1), ("near", 0), ("near", 1))


def z_index(z):
    return (z % 2) * 4 + z // 2


def z_perm(even, odd):
    return [(z_index(z), z_index((z + (odd if z % 2 else even)) % 8)) for z in range(8)]


TO = (z_perm(-1, 1), z_perm(2, -2), z_perm(-3, 3))
BACK = (z_perm(-1, 1), z_perm(-2, 2), z_perm(-3, 3))
PAIR = z_perm(1, -1)
SWAP = [(0, 1), (1, 0)]
AROUND_X = [[(i, (i + k) % 4) for i in range(4)] for k in (1, 3, 2)]


def spec(shape, index_map=None):
    return pl.BlockSpec(shape, index_map) if index_map else pl.BlockSpec(memory_space=pltpu.VMEM)


def pack_body(offs, *refs):
    sources, outs, held, sems = refs[:6], refs[6:-7], refs[-7:-1], refs[-1]
    copies = [pltpu.make_async_copy(a, b, sems.at[i]) for i, (a, b) in enumerate(zip(sources, held))]
    for copy in copies:
        copy.start()
    for a in range(6):
        copies[a].wait()
        for slot in range(4):
            for h in range(HEADS_HERE):
                col = pl.multiple_of(offs[slot] + h * HEAD_DIM, HEAD_DIM)
                block = held[a][:, pl.ds(col, HEAD_DIM)]
                if a < 4:
                    outs[slot][h * 4 + a] = block
                elif slot == 1:
                    outs[slot][KV_BLOCKS + h * 2 + a - 4] = block
                else:
                    outs[4 + slot // 2 + slot // 3][h * 2 + a - 4] = block


def pack(offs, arrays):
    block = lambda count: jax.ShapeDtypeStruct((count, ROWS, HEAD_DIM), jnp.bfloat16)
    return pl.pallas_call(
        pack_body,
        out_shape=[block(KV_BLOCKS), block(KV_BLOCKS + Q_BLOCKS)]
        + [block(KV_BLOCKS)] * 2
        + [block(Q_BLOCKS)] * 3,
        in_specs=[pl.BlockSpec(memory_space=pltpu.SMEM)] + [pl.BlockSpec(memory_space=pl.ANY)] * 6,
        out_specs=[spec(None)] * 7,
        scratch_shapes=[pltpu.VMEM(arrays[0].shape, jnp.bfloat16)] * 6
        + [pltpu.SemaphoreType.DMA((6,))],
        compiler_params=pltpu.CompilerParams(vmem_limit_bytes=60 * 1024 * 1024),
        name="pack",
    )(offs, *arrays)


def unpack_body(chunk, offs, *refs):
    low, high = CHUNKS[chunk]
    pieces, before, (out, out_tan) = refs[:4], refs[4:-2], refs[-2:]
    if before:
        out[...] = before[0][...]
        out_tan[...] = before[1][...]
    for slot, ref in enumerate(pieces):
        for h in range(low, high):
            col = pl.multiple_of(offs[slot] + h * HEAD_DIM, HEAD_DIM)
            out[:, pl.ds(col, HEAD_DIM)] = ref[h - low, 0]
            out_tan[:, pl.ds(col, HEAD_DIM)] = ref[h - low, 1]


def unpack(chunk, offs, pieces, before):
    shape = jax.ShapeDtypeStruct((ROWS, GROUPS * HEADS_HERE * HEAD_DIM), jnp.bfloat16)
    return pl.pallas_call(
        functools.partial(unpack_body, chunk),
        out_shape=[shape, shape],
        in_specs=[pl.BlockSpec(memory_space=pltpu.SMEM)] + [spec(None)] * (4 + len(before)),
        out_specs=[spec(None)] * 2,
        compiler_params=pltpu.CompilerParams(vmem_limit_bytes=VMEM),
        name="unpack",
    )(offs, *pieces, *before)


def fold(block):
    return block.reshape(block.shape[0] * block.shape[1], block.shape[2])


def core_part(q_ref, kv_refs, kk, vv):
    row = 0
    for ref in kv_refs:
        rows = pl.ds(row, ROWS)
        row += ROWS
        kk[rows, :HEAD_DIM] = ref[0]
        kk[rows, HEAD_DIM:] = ref[2]
        vv[rows, :HEAD_DIM] = ref[1]
        vv[rows, HEAD_DIM:] = ref[3]
    q, dq = fold(q_ref[:, 0]), fold(q_ref[:, 1])
    nt = (((1,), (1,)), ((), ()))
    dot = functools.partial(lax.dot_general, preferred_element_type=jnp.float32)
    s = dot(q, kk[:, :HEAD_DIM], nt)
    st = dot(jnp.concatenate([dq, q], axis=1), kk[...], nt)
    m = jnp.max(s, axis=1, keepdims=True)
    p = jnp.exp2((s - m) * (SCALE * LOG2E))
    t = p * st
    total = jnp.sum(p, axis=1, keepdims=True)
    slope = jnp.sum(t, axis=1, keepdims=True)
    nn = (((1,), (0,)), ((), ()))
    pv = dot(p.astype(jnp.bfloat16), vv[...], nn)
    tv = dot(t.astype(jnp.bfloat16), vv[:, :HEAD_DIM], nn)
    inverse = 1.0 / total
    att = pv[:, :HEAD_DIM] * inverse
    slope = slope * (inverse * SCALE)
    tan = (pv[:, HEAD_DIM:] + tv * SCALE) * inverse - att * slope
    return att, tan, m * SCALE + jnp.log(total), slope


def three(value):
    high = value.astype(jnp.bfloat16).astype(jnp.float32)
    rest = value - high
    middle = rest.astype(jnp.bfloat16).astype(jnp.float32)
    return high, middle, rest - middle


def far_body(count, *refs):
    q_ref, kv_refs, (out, kk, vv) = refs[0], refs[1 : 1 + count], refs[1 + count :]
    att, tan, lse, slope = core_part(q_ref, kv_refs, kk, vv)
    n = att.shape[0]
    out[0, :n] = att.astype(jnp.bfloat16)
    out[0, n : 2 * n] = tan.astype(jnp.bfloat16)
    lane = lax.broadcasted_iota(jnp.int32, (n, HEAD_DIM), 1)
    stats = jnp.zeros((n, HEAD_DIM), jnp.float32)
    for i, column in enumerate(three(lse) + three(slope)):
        stats = jnp.where(lane == i, column, stats)
    flat = jnp.transpose(stats)[:16].astype(jnp.bfloat16)
    out[0, 2 * n : 2 * n + 16] = flat[:, :HEAD_DIM]
    out[0, 2 * n + 16 :] = flat[:, HEAD_DIM:]


def near_body(count, *refs):
    q_ref, kv_refs, got = refs[0], refs[1 : 1 + count], refs[1 + count]
    outs, (kk, vv) = refs[2 + count : 6 + count], refs[6 + count :]
    att, tan, lse, slope = core_part(q_ref, kv_refs, kk, vv)
    n = att.shape[0]
    att2 = got[0, :n].astype(jnp.float32)
    tan2 = got[0, n : 2 * n].astype(jnp.float32)
    flat = jnp.concatenate([got[0, 2 * n : 2 * n + 16], got[0, 2 * n + 16 :]], axis=1)
    flat = flat.astype(jnp.float32)

    def column(i):
        line = flat[i : i + 1] + flat[i + 1 : i + 2] + flat[i + 2 : i + 3]
        return jnp.transpose(jnp.broadcast_to(line, (HEAD_DIM, n)))

    lse2, slope2 = column(0), column(3)
    w1 = 1.0 / (1.0 + jnp.exp(lse2 - lse))
    w2 = 1.0 / (1.0 + jnp.exp(lse - lse2))
    tan = w1 * tan + w2 * tan2 + (w1 * w2) * (slope - slope2) * (att - att2)
    att = w1 * att + w2 * att2
    for slot in range(4):
        rows = slice(slot * ROWS, (slot + 1) * ROWS)
        outs[slot][0, 0] = att[rows].astype(jnp.bfloat16)
        outs[slot][0, 1] = tan[rows].astype(jnp.bfloat16)


def attend(q, pieces, low, high, got=None):
    heads = high - low
    keys = len(pieces) * ROWS
    rows = 4 * ROWS
    in_specs = [pl.BlockSpec((4, 2, ROWS, HEAD_DIM), lambda h: (0, h + low, 0, 0))]
    for _, i in pieces:
        in_specs.append(
            pl.BlockSpec((4, ROWS, HEAD_DIM), lambda h, i=i: (h + low + i * HEADS_HERE, 0, 0))
        )
    args = [q] + [p for p, _ in pieces]
    wide = 2 * rows + 32
    if got is None:
        body = functools.partial(far_body, len(pieces))
        out_shape = jax.ShapeDtypeStruct((heads, wide, HEAD_DIM), jnp.bfloat16)
        out_specs = pl.BlockSpec((1, wide, HEAD_DIM), lambda h: (h, 0, 0))
    else:
        body = functools.partial(near_body, len(pieces))
        args.append(got)
        in_specs.append(pl.BlockSpec((1, wide, HEAD_DIM), lambda h: (h, 0, 0)))
        out_shape = [jax.ShapeDtypeStruct((heads, 2, ROWS, HEAD_DIM), jnp.bfloat16)] * 4
        out_specs = [pl.BlockSpec((1, 2, ROWS, HEAD_DIM), lambda h: (h, 0, 0, 0))] * 4
    return pl.pallas_call(
        body,
        grid=(heads,),
        out_shape=out_shape,
        in_specs=in_specs,
        out_specs=out_specs,
        scratch_shapes=[pltpu.VMEM((keys, 2 * HEAD_DIM), jnp.bfloat16)] * 2,
        compiler_params=pltpu.CompilerParams(vmem_limit_bytes=VMEM),
        cost_estimate=pl.CostEstimate(
            flops=16 * heads * rows * keys * HEAD_DIM,
            bytes_accessed=heads * keys * 4 * HEAD_DIM * 2,
            transcendentals=heads * rows * keys,
        ),
        name="far_rows" if got is None else "near_rows",
    )(*args)


def after(value, *needed):
    return lax.optimization_barrier((value, *needed))[0]


def per_device(query_rows, key_rows, value_rows, query_tan, key_tan, value_tan):
    group, parity = lax.axis_index("zhi"), lax.axis_index("zlo")
    step = 2 * parity - 1
    slots = jnp.stack([group, group + step, group - step, group + 2]) % GROUPS
    offs = (slots * (HEADS_HERE * HEAD_DIM)).astype(jnp.int32)
    own, to_one, to_two, to_three, own_q, to_two_q, to_three_q = pack(
        offs, (key_rows, value_rows, key_tan, value_tan, query_rows, query_tan)
    )
    around = lambda array: [lax.ppermute(array, "x", perm) for perm in AROUND_X]
    swap = lambda arrays: [lax.ppermute(a, "core", SWAP) for a in arrays]
    one = lax.ppermute(to_one, Z, TO[0])
    two_q = lax.ppermute(to_two_q, Z, TO[1])
    own_x = around(own)
    one, two_q, own, own_x, to_two, to_three_q, to_three = lax.optimization_barrier(
        (one, two_q, own, own_x, to_two, to_three_q, to_three)
    )
    one, one_q = one[:KV_BLOCKS], one[KV_BLOCKS:]
    two = lax.ppermute(to_two, Z, TO[1])
    three_q = lax.ppermute(to_three_q, Z, TO[2])
    one_x = around(one)
    two, three_q, one, one_x, own, own_x, to_three = lax.optimization_barrier(
        (two, three_q, one, one_x, own, own_x, to_three)
    )
    three_ = lax.ppermute(to_three, Z, TO[2])
    two_x = around(two)
    own_s = lax.ppermute(jnp.concatenate([own, *own_x]), "core", SWAP)
    near_q = jnp.stack([own_q, one_q, two_q, three_q])
    three_, two, two_x, one, one_x, own_s, near_q = lax.optimization_barrier(
        (three_, two, two_x, one, one_x, own_s, near_q)
    )
    three_x = around(three_)
    far_q = lax.ppermute(near_q, Z, PAIR)
    both_s = lax.ppermute(jnp.concatenate([one, *one_x, two, *two_x]), "core", SWAP)
    three_, three_x, both_s, far_q = lax.optimization_barrier((three_, three_x, both_s, far_q))
    three_s = swap([three_, *three_x])
    pieces = [(p, 0) for p in (own, *own_x, one, *one_x, two, *two_x, three_, *three_x, *three_s)]
    pieces += [(own_s, i) for i in range(4)] + [(both_s, i) for i in range(8)]
    sent, got, result, last, back = {}, {}, (), (), []
    for kind, c in ORDER:
        low, high = CHUNKS[c]
        if kind == "far":
            sent[c] = attend(after(far_q, *last), pieces, low, high)
            got[c] = lax.ppermute(sent[c], Z, PAIR)
            last = (sent[c],)
        else:
            near = attend(after(near_q, *last), pieces, low, high, got[c])
            if back:
                result = unpack(c - 1, offs, [after(back[0], *near), *back[1:]], result)
            back = [near[0]]
            back += [lax.ppermute(after(o, *result), Z, perm) for o, perm in zip(near[1:], BACK)]
            last = (near[0],)
    return tuple(unpack(len(CHUNKS) - 1, offs, back, result))


def solution(mesh):
    fine = Mesh(mesh.devices.reshape(4, 2, 4, 2, 4), AXES)
    rows = P(AXES, None)
    return jax.shard_map(
        per_device,
        mesh=fine,
        in_specs=(rows,) * 6,
        out_specs=(rows, rows),
        check_vma=False,
    )
```

```python
import functools

import jax
import jax.numpy as jnp
from jax import lax
from jax.experimental import pallas as pl
from jax.experimental.pallas import tpu as pltpu
from jax.sharding import Mesh
from jax.sharding import PartitionSpec as P

HEAD_DIM = 128
HEADS_HERE = 5
GROUPS = 4
ROWS = 64
KV_BLOCKS, Q_BLOCKS = 4 * HEADS_HERE, 2 * HEADS_HERE
AXES = ("clip", "zlo", "x", "core", "zhi")
Z = ("zlo", "zhi")
SCALE = HEAD_DIM**-0.5
LOG2E = 1.4426950408889634
CHUNKS = ((0, 2), (2, 5))
VMEM = 40 * 1024 * 1024
ORDER = (("far", 0), ("far", 1), ("near", 0), ("near", 1))


def z_index(z):
    return (z % 2) * 4 + z // 2


def z_perm(even, odd):
    return [(z_index(z), z_index((z + (odd if z % 2 else even)) % 8)) for z in range(8)]


TO = (z_perm(-1, 1), z_perm(2, -2), z_perm(-3, 3))
BACK = (z_perm(-1, 1), z_perm(-2, 2), z_perm(-3, 3))
PAIR = z_perm(1, -1)
SWAP = [(0, 1), (1, 0)]
AROUND_X = [[(i, (i + k) % 4) for i in range(4)] for k in (1, 3, 2)]


def spec(shape, index_map=None):
    return pl.BlockSpec(shape, index_map) if index_map else pl.BlockSpec(memory_space=pltpu.VMEM)


def pack_body(offs, *refs):
    sources, outs, held, sems = refs[:6], refs[6:-7], refs[-7:-1], refs[-1]
    copies = [pltpu.make_async_copy(a, b, sems.at[i]) for i, (a, b) in enumerate(zip(sources, held))]
    for copy in copies:
        copy.start()
    for a in range(6):
        copies[a].wait()
        for slot in range(4):
            for h in range(HEADS_HERE):
                col = pl.multiple_of(offs[slot] + h * HEAD_DIM, HEAD_DIM)
                block = held[a][:, pl.ds(col, HEAD_DIM)]
                if a < 4:
                    outs[slot][h * 4 + a] = block
                elif slot == 1:
                    outs[slot][KV_BLOCKS + h * 2 + a - 4] = block
                else:
                    outs[4 + slot // 2 + slot // 3][h * 2 + a - 4] = block


def pack(offs, arrays):
    block = lambda count: jax.ShapeDtypeStruct((count, ROWS, HEAD_DIM), jnp.bfloat16)
    return pl.pallas_call(
        pack_body,
        out_shape=[block(KV_BLOCKS), block(KV_BLOCKS + Q_BLOCKS)]
        + [block(KV_BLOCKS)] * 2
        + [block(Q_BLOCKS)] * 3,
        in_specs=[pl.BlockSpec(memory_space=pltpu.SMEM)] + [pl.BlockSpec(memory_space=pl.ANY)] * 6,
        out_specs=[spec(None)] * 7,
        scratch_shapes=[pltpu.VMEM(arrays[0].shape, jnp.bfloat16)] * 6
        + [pltpu.SemaphoreType.DMA((6,))],
        compiler_params=pltpu.CompilerParams(vmem_limit_bytes=60 * 1024 * 1024),
        name="pack",
    )(offs, *arrays)


def unpack_body(chunk, offs, *refs):
    low, high = CHUNKS[chunk]
    pieces, before, (out, out_tan) = refs[:4], refs[4:-2], refs[-2:]
    if before:
        out[...] = before[0][...]
        out_tan[...] = before[1][...]
    for slot, ref in enumerate(pieces):
        for h in range(low, high):
            col = pl.multiple_of(offs[slot] + h * HEAD_DIM, HEAD_DIM)
            out[:, pl.ds(col, HEAD_DIM)] = ref[h - low, 0]
            out_tan[:, pl.ds(col, HEAD_DIM)] = ref[h - low, 1]


def unpack(chunk, offs, pieces, before):
    shape = jax.ShapeDtypeStruct((ROWS, GROUPS * HEADS_HERE * HEAD_DIM), jnp.bfloat16)
    return pl.pallas_call(
        functools.partial(unpack_body, chunk),
        out_shape=[shape, shape],
        in_specs=[pl.BlockSpec(memory_space=pltpu.SMEM)] + [spec(None)] * (4 + len(before)),
        out_specs=[spec(None)] * 2,
        compiler_params=pltpu.CompilerParams(vmem_limit_bytes=VMEM),
        name="unpack",
    )(offs, *pieces, *before)


def fold(block):
    return block.reshape(block.shape[0] * block.shape[1], block.shape[2])


def load_keys(kv_refs, kk, vv):
    row = 0
    for ref in kv_refs:
        rows = pl.ds(row, ROWS)
        row += ROWS
        kk[rows, :HEAD_DIM] = ref[0]
        kk[rows, HEAD_DIM:] = ref[2]
        vv[rows, :HEAD_DIM] = ref[1]
        vv[rows, HEAD_DIM:] = ref[3]


def core_part(q_ref, kk, vv):
    q, dq = fold(q_ref[:, 0]), fold(q_ref[:, 1])
    nt = (((1,), (1,)), ((), ()))
    dot = functools.partial(lax.dot_general, preferred_element_type=jnp.float32)
    s = dot(q, kk[:, :HEAD_DIM], nt)
    st = dot(jnp.concatenate([dq, q], axis=1), kk[...], nt)
    m = jnp.max(s, axis=1, keepdims=True)
    p = jnp.exp2((s - m) * (SCALE * LOG2E))
    t = p * st
    total = jnp.sum(p, axis=1, keepdims=True)
    slope = jnp.sum(t, axis=1, keepdims=True)
    nn = (((1,), (0,)), ((), ()))
    pv = dot(p.astype(jnp.bfloat16), vv[...], nn)
    tv = dot(t.astype(jnp.bfloat16), vv[:, :HEAD_DIM], nn)
    inverse = 1.0 / total
    att = pv[:, :HEAD_DIM] * inverse
    slope = slope * (inverse * SCALE)
    tan = (pv[:, HEAD_DIM:] + tv * SCALE) * inverse - att * slope
    return att, tan, m * SCALE + jnp.log(total), slope


def three(value):
    high = value.astype(jnp.bfloat16).astype(jnp.float32)
    rest = value - high
    middle = rest.astype(jnp.bfloat16).astype(jnp.float32)
    return high, middle, rest - middle


def write_part(out, part):
    att, tan, lse, slope = part
    n = att.shape[0]
    out[:n] = att.astype(jnp.bfloat16)
    out[n : 2 * n] = tan.astype(jnp.bfloat16)
    lane = lax.broadcasted_iota(jnp.int32, (n, HEAD_DIM), 1)
    stats = jnp.zeros((n, HEAD_DIM), jnp.float32)
    for i, column in enumerate(three(lse) + three(slope)):
        stats = jnp.where(lane == i, column, stats)
    flat = jnp.transpose(stats)[:16].astype(jnp.bfloat16)
    out[2 * n : 2 * n + 16] = flat[:, :HEAD_DIM]
    out[2 * n + 16 :] = flat[:, HEAD_DIM:]


def merge(part, got):
    att, tan, lse, slope = part
    n = att.shape[0]
    att2 = got[:n].astype(jnp.float32)
    tan2 = got[n : 2 * n].astype(jnp.float32)
    flat = jnp.concatenate([got[2 * n : 2 * n + 16], got[2 * n + 16 :]], axis=1)
    flat = flat.astype(jnp.float32)

    def column(i):
        line = flat[i : i + 1] + flat[i + 1 : i + 2] + flat[i + 2 : i + 3]
        return jnp.transpose(jnp.broadcast_to(line, (HEAD_DIM, n)))

    lse2, slope2 = column(0), column(3)
    w1 = 1.0 / (1.0 + jnp.exp(lse2 - lse))
    w2 = 1.0 / (1.0 + jnp.exp(lse - lse2))
    top = jnp.maximum(lse, lse2)
    return (
        w1 * att + w2 * att2,
        w1 * tan + w2 * tan2 + (w1 * w2) * (slope - slope2) * (att - att2),
        top + jnp.log(jnp.exp(lse - top) + jnp.exp(lse2 - top)),
        w1 * slope + w2 * slope2,
    )


def attend_body(q_count, got_count, piece_count, *refs):
    refs = list(refs)
    take = lambda n: [refs.pop(0) for _ in range(n)]
    q_refs, got_refs, kv_refs = take(q_count), take(got_count), take(piece_count)
    kk, vv = refs.pop(-2), refs.pop(-1)
    load_keys(kv_refs, kk, vv)
    for i, q_ref in enumerate(q_refs):
        part = core_part(q_ref, kk, vv)
        for got in got_refs:
            part = merge(part, got.at[0, 0])
        if len(refs) == 1:
            write_part(refs[0].at[0, i], part)
        else:
            for slot in range(4):
                rows = slice(slot * ROWS, (slot + 1) * ROWS)
                refs[slot][0, 0] = part[0][rows].astype(jnp.bfloat16)
                refs[slot][0, 1] = part[1][rows].astype(jnp.bfloat16)


def attend(name, qs, pieces, chunk, gots=(), last=False):
    low, high = chunk
    heads = high - low
    keys = len(pieces) * ROWS
    rows = 4 * ROWS
    wide = 2 * rows + 32
    in_specs = [pl.BlockSpec((4, 2, ROWS, HEAD_DIM), lambda h: (0, h + low, 0, 0))] * len(qs)
    for _, start, which in gots:
        in_specs.append(
            pl.BlockSpec(
                (1, 1, wide, HEAD_DIM), lambda h, n=low - start, i=which: (h + n, i, 0, 0)
            )
        )
    for _, i in pieces:
        in_specs.append(
            pl.BlockSpec((4, ROWS, HEAD_DIM), lambda h, i=i: (h + low + i * HEADS_HERE, 0, 0))
        )
    if last:
        out_shape = [jax.ShapeDtypeStruct((heads, 2, ROWS, HEAD_DIM), jnp.bfloat16)] * 4
        out_specs = [pl.BlockSpec((1, 2, ROWS, HEAD_DIM), lambda h: (h, 0, 0, 0))] * 4
    else:
        out_shape = jax.ShapeDtypeStruct((heads, len(qs), wide, HEAD_DIM), jnp.bfloat16)
        out_specs = pl.BlockSpec((1, len(qs), wide, HEAD_DIM), lambda h: (h, 0, 0, 0))
    return pl.pallas_call(
        functools.partial(attend_body, len(qs), len(gots), len(pieces)),
        grid=(heads,),
        out_shape=out_shape,
        in_specs=in_specs,
        out_specs=out_specs,
        scratch_shapes=[pltpu.VMEM((keys, 2 * HEAD_DIM), jnp.bfloat16)] * 2,
        compiler_params=pltpu.CompilerParams(vmem_limit_bytes=VMEM),
        cost_estimate=pl.CostEstimate(
            flops=16 * len(qs) * heads * rows * keys * HEAD_DIM,
            bytes_accessed=heads * keys * 4 * HEAD_DIM * 2,
            transcendentals=len(qs) * heads * rows * keys,
        ),
        name=name,
    )(*qs, *[array for array, _, _ in gots], *[p for p, _ in pieces])


def after(value, *needed):
    return lax.optimization_barrier((value, *needed))[0]


def per_device(query_rows, key_rows, value_rows, query_tan, key_tan, value_tan):
    group, parity = lax.axis_index("zhi"), lax.axis_index("zlo")
    step = 2 * parity - 1
    slots = jnp.stack([group, group + step, group - step, group + 2]) % GROUPS
    offs = (slots * (HEADS_HERE * HEAD_DIM)).astype(jnp.int32)
    own, to_one, to_two, to_three, own_q, to_two_q, to_three_q = pack(
        offs, (key_rows, value_rows, key_tan, value_tan, query_rows, query_tan)
    )
    around = lambda array: [lax.ppermute(array, "x", perm) for perm in AROUND_X]
    swap = lambda arrays: [lax.ppermute(a, "core", SWAP) for a in arrays]
    one = lax.ppermute(to_one, Z, TO[0])
    two_q = lax.ppermute(to_two_q, Z, TO[1])
    own_x = around(own)
    one, two_q, own, own_x, to_two, to_three_q, to_three = lax.optimization_barrier(
        (one, two_q, own, own_x, to_two, to_three_q, to_three)
    )
    one, one_q = one[:KV_BLOCKS], one[KV_BLOCKS:]
    two = lax.ppermute(to_two, Z, TO[1])
    three_q = lax.ppermute(to_three_q, Z, TO[2])
    one_x = around(one)
    two, three_q, one, one_x, own, own_x, to_three = lax.optimization_barrier(
        (two, three_q, one, one_x, own, own_x, to_three)
    )
    three_ = lax.ppermute(to_three, Z, TO[2])
    two_x = around(two)
    own_s = lax.ppermute(jnp.concatenate([own, *own_x]), "core", SWAP)
    near_q = jnp.stack([own_q, one_q, two_q, three_q])
    three_, two, two_x, one, one_x, own_s, near_q = lax.optimization_barrier(
        (three_, two, two_x, one, one_x, own_s, near_q)
    )
    three_x = around(three_)
    far_q = lax.ppermute(near_q, Z, PAIR)
    both_s = lax.ppermute(jnp.concatenate([one, *one_x, two, *two_x]), "core", SWAP)
    pieces = [(p, 0) for p in (own, *own_x, one, *one_x, two, *two_x)]
    pieces += [(own_s, i) for i in range(4)] + [(both_s, i) for i in range(8)]
    early = attend("early", [near_q], pieces, (0, HEADS_HERE))
    three_, three_x, far_q, early = lax.optimization_barrier((three_, three_x, far_q, early))
    three_s = swap([three_, *three_x])
    late = [(p, 0) for p in (three_, *three_x, *three_s)]
    early_far = attend("early_far", [far_q], pieces, CHUNKS[0])
    paired, result, last, back = {}, (), (), []
    for kind, c in ORDER:
        chunk = CHUNKS[c]
        if kind == "far":
            if c == 0:
                part = attend(kind, [far_q], late, chunk, [(early_far, chunk[0], 0)])
            else:
                part = attend(kind, [after(far_q, *last)], pieces + late, chunk)
            paired[c] = lax.ppermute(after(part, *paired.values()), Z, PAIR)
            last = (part,)
        else:
            gots = [(early, 0, 0), (paired[c], chunk[0], 0)]
            near = attend(kind, [after(near_q, *last)], late, chunk, gots, last=True)
            if back:
                result = unpack(c - 1, offs, [after(back[0], *near), *back[1:]], result)
            back = [near[0]]
            back += [lax.ppermute(after(o, *result), Z, perm) for o, perm in zip(near[1:], BACK)]
            last = (near[0],)
    return tuple(unpack(len(CHUNKS) - 1, offs, back, result))


def solution(mesh):
    fine = Mesh(mesh.devices.reshape(4, 2, 4, 2, 4), AXES)
    rows = P(AXES, None)
    return jax.shard_map(
        per_device,
        mesh=fine,
        in_specs=(rows,) * 6,
        out_specs=(rows, rows),
        check_vma=False,
    )
```

```python
import functools

import jax
import jax.numpy as jnp
from jax import lax
from jax.experimental import pallas as pl
from jax.experimental.pallas import tpu as pltpu
from jax.sharding import Mesh
from jax.sharding import PartitionSpec as P

HEAD_DIM = 128
HEADS_HERE = 5
GROUPS = 4
ROWS = 64
KV_BLOCKS, Q_BLOCKS = 4 * HEADS_HERE, 2 * HEADS_HERE
AXES = ("clip", "zlo", "x", "core", "zhi")
Z = ("zlo", "zhi")
SCALE = HEAD_DIM**-0.5
LOG2E = 1.4426950408889634
CHUNKS = ((0, 2), (2, 5))
VMEM = 40 * 1024 * 1024
ORDER = (("far", 0), ("far", 1), ("near", 0), ("near", 1))


def z_index(z):
    return (z % 2) * 4 + z // 2


def z_perm(even, odd):
    return [(z_index(z), z_index((z + (odd if z % 2 else even)) % 8)) for z in range(8)]


TO = (z_perm(-1, 1), z_perm(2, -2), z_perm(-3, 3))
BACK = (z_perm(-1, 1), z_perm(-2, 2), z_perm(-3, 3))
PAIR = z_perm(1, -1)
SWAP = [(0, 1), (1, 0)]
AROUND_X = [[(i, (i + k) % 4) for i in range(4)] for k in (1, 3, 2)]


def spec(shape, index_map=None):
    return pl.BlockSpec(shape, index_map) if index_map else pl.BlockSpec(memory_space=pltpu.VMEM)


def offsets():
    group, parity = lax.axis_index("zhi"), lax.axis_index("zlo")
    step = 2 * parity - 1
    slots = (group, group + step + GROUPS, group - step + GROUPS, group + 2)
    return [lax.rem(slot, GROUPS) * (HEADS_HERE * HEAD_DIM) for slot in slots]


def pack_body(*refs):
    offs = offsets()
    sources, outs, held, sems = refs[:6], refs[6:-7], refs[-7:-1], refs[-1]
    copies = [pltpu.make_async_copy(a, b, sems.at[i]) for i, (a, b) in enumerate(zip(sources, held))]
    for copy in copies:
        copy.start()
    for a in range(6):
        copies[a].wait()
        for slot in range(4):
            for h in range(HEADS_HERE):
                col = pl.multiple_of(offs[slot] + h * HEAD_DIM, HEAD_DIM)
                block = held[a][:, pl.ds(col, HEAD_DIM)]
                if a < 4:
                    outs[slot][h * 4 + a] = block
                elif slot == 1:
                    outs[slot][KV_BLOCKS + h * 2 + a - 4] = block
                else:
                    outs[4 + slot // 2 + slot // 3][h * 2 + a - 4] = block


def pack(arrays):
    block = lambda count: jax.ShapeDtypeStruct((count, ROWS, HEAD_DIM), jnp.bfloat16)
    return pl.pallas_call(
        pack_body,
        out_shape=[block(KV_BLOCKS), block(KV_BLOCKS + Q_BLOCKS)]
        + [block(KV_BLOCKS)] * 2
        + [block(Q_BLOCKS)] * 3,
        in_specs=[pl.BlockSpec(memory_space=pl.ANY)] * 6,
        out_specs=[spec(None)] * 7,
        scratch_shapes=[pltpu.VMEM(arrays[0].shape, jnp.bfloat16)] * 6
        + [pltpu.SemaphoreType.DMA((6,))],
        compiler_params=pltpu.CompilerParams(vmem_limit_bytes=60 * 1024 * 1024),
        name="pack",
    )(*arrays)


def unpack_body(chunk, offs, *refs):
    low, high = CHUNKS[chunk]
    pieces, before, (out, out_tan) = refs[:4], refs[4:-2], refs[-2:]
    if before:
        out[...] = before[0][...]
        out_tan[...] = before[1][...]
    for slot, ref in enumerate(pieces):
        for h in range(low, high):
            col = pl.multiple_of(offs[slot] + h * HEAD_DIM, HEAD_DIM)
            out[:, pl.ds(col, HEAD_DIM)] = ref[h - low, 0]
            out_tan[:, pl.ds(col, HEAD_DIM)] = ref[h - low, 1]


def unpack(chunk, offs, pieces, before):
    shape = jax.ShapeDtypeStruct((ROWS, GROUPS * HEADS_HERE * HEAD_DIM), jnp.bfloat16)
    return pl.pallas_call(
        functools.partial(unpack_body, chunk),
        out_shape=[shape, shape],
        in_specs=[pl.BlockSpec(memory_space=pltpu.SMEM)] + [spec(None)] * (4 + len(before)),
        out_specs=[spec(None)] * 2,
        compiler_params=pltpu.CompilerParams(vmem_limit_bytes=VMEM),
        name="unpack",
    )(offs, *pieces, *before)


def fold(block):
    return block.reshape(block.shape[0] * block.shape[1], block.shape[2])


def load_keys(kv_refs, kk, vv):
    row = 0
    for ref in kv_refs:
        rows = pl.ds(row, ROWS)
        row += ROWS
        kk[rows, :HEAD_DIM] = ref[0]
        kk[rows, HEAD_DIM:] = ref[2]
        vv[rows, :HEAD_DIM] = ref[1]
        vv[rows, HEAD_DIM:] = ref[3]


def core_part(q_ref, kk, vv):
    q, dq = fold(q_ref[:, 0]), fold(q_ref[:, 1])
    nt = (((1,), (1,)), ((), ()))
    dot = functools.partial(lax.dot_general, preferred_element_type=jnp.float32)
    s = dot(q, kk[:, :HEAD_DIM], nt)
    st = dot(jnp.concatenate([dq, q], axis=1), kk[...], nt)
    m = jnp.max(s, axis=1, keepdims=True)
    p = jnp.exp2((s - m) * (SCALE * LOG2E))
    t = p * st
    total = jnp.sum(p, axis=1, keepdims=True)
    slope = jnp.sum(t, axis=1, keepdims=True)
    nn = (((1,), (0,)), ((), ()))
    pv = dot(p.astype(jnp.bfloat16), vv[...], nn)
    tv = dot(t.astype(jnp.bfloat16), vv[:, :HEAD_DIM], nn)
    inverse = 1.0 / total
    att = pv[:, :HEAD_DIM] * inverse
    slope = slope * (inverse * SCALE)
    tan = (pv[:, HEAD_DIM:] + tv * SCALE) * inverse - att * slope
    return att, tan, m * SCALE + jnp.log(total), slope


def three(value):
    high = value.astype(jnp.bfloat16).astype(jnp.float32)
    rest = value - high
    middle = rest.astype(jnp.bfloat16).astype(jnp.float32)
    return high, middle, rest - middle


def write_part(out, part):
    att, tan, lse, slope = part
    n = att.shape[0]
    out[:n] = att.astype(jnp.bfloat16)
    out[n : 2 * n] = tan.astype(jnp.bfloat16)
    lane = lax.broadcasted_iota(jnp.int32, (n, HEAD_DIM), 1)
    stats = jnp.zeros((n, HEAD_DIM), jnp.float32)
    for i, column in enumerate(three(lse) + three(slope)):
        stats = jnp.where(lane == i, column, stats)
    flat = jnp.transpose(stats)[:16].astype(jnp.bfloat16)
    out[2 * n : 2 * n + 16] = flat[:, :HEAD_DIM]
    out[2 * n + 16 :] = flat[:, HEAD_DIM:]


def merge(part, got):
    att, tan, lse, slope = part
    n = att.shape[0]
    att2 = got[:n].astype(jnp.float32)
    tan2 = got[n : 2 * n].astype(jnp.float32)
    flat = jnp.concatenate([got[2 * n : 2 * n + 16], got[2 * n + 16 :]], axis=1)
    flat = flat.astype(jnp.float32)

    def column(i):
        line = flat[i : i + 1] + flat[i + 1 : i + 2] + flat[i + 2 : i + 3]
        return jnp.transpose(jnp.broadcast_to(line, (HEAD_DIM, n)))

    lse2, slope2 = column(0), column(3)
    w1 = 1.0 / (1.0 + jnp.exp(lse2 - lse))
    w2 = 1.0 / (1.0 + jnp.exp(lse - lse2))
    top = jnp.maximum(lse, lse2)
    return (
        w1 * att + w2 * att2,
        w1 * tan + w2 * tan2 + (w1 * w2) * (slope - slope2) * (att - att2),
        top + jnp.log(jnp.exp(lse - top) + jnp.exp(lse2 - top)),
        w1 * slope + w2 * slope2,
    )


def attend_body(q_count, got_count, piece_count, *refs):
    refs = list(refs)
    take = lambda n: [refs.pop(0) for _ in range(n)]
    q_refs, got_refs, kv_refs = take(q_count), take(got_count), take(piece_count)
    kk, vv = refs.pop(-2), refs.pop(-1)
    load_keys(kv_refs, kk, vv)
    for i, q_ref in enumerate(q_refs):
        part = core_part(q_ref, kk, vv)
        for got in got_refs:
            part = merge(part, got.at[0, 0])
        if len(refs) == 1:
            write_part(refs[0].at[0, i], part)
        else:
            for slot in range(4):
                rows = slice(slot * ROWS, (slot + 1) * ROWS)
                refs[slot][0, 0] = part[0][rows].astype(jnp.bfloat16)
                refs[slot][0, 1] = part[1][rows].astype(jnp.bfloat16)


def attend(name, qs, pieces, chunk, gots=(), last=False):
    low, high = chunk
    heads = high - low
    keys = len(pieces) * ROWS
    rows = 4 * ROWS
    wide = 2 * rows + 32
    in_specs = [pl.BlockSpec((4, 2, ROWS, HEAD_DIM), lambda h: (0, h + low, 0, 0))] * len(qs)
    for _, start, which in gots:
        in_specs.append(
            pl.BlockSpec(
                (1, 1, wide, HEAD_DIM), lambda h, n=low - start, i=which: (h + n, i, 0, 0)
            )
        )
    for _, i in pieces:
        in_specs.append(
            pl.BlockSpec((4, ROWS, HEAD_DIM), lambda h, i=i: (h + low + i * HEADS_HERE, 0, 0))
        )
    if last:
        out_shape = [jax.ShapeDtypeStruct((heads, 2, ROWS, HEAD_DIM), jnp.bfloat16)] * 4
        out_specs = [pl.BlockSpec((1, 2, ROWS, HEAD_DIM), lambda h: (h, 0, 0, 0))] * 4
    else:
        out_shape = jax.ShapeDtypeStruct((heads, len(qs), wide, HEAD_DIM), jnp.bfloat16)
        out_specs = pl.BlockSpec((1, len(qs), wide, HEAD_DIM), lambda h: (h, 0, 0, 0))
    return pl.pallas_call(
        functools.partial(attend_body, len(qs), len(gots), len(pieces)),
        grid=(heads,),
        out_shape=out_shape,
        in_specs=in_specs,
        out_specs=out_specs,
        scratch_shapes=[pltpu.VMEM((keys, 2 * HEAD_DIM), jnp.bfloat16)] * 2,
        compiler_params=pltpu.CompilerParams(vmem_limit_bytes=VMEM),
        cost_estimate=pl.CostEstimate(
            flops=16 * len(qs) * heads * rows * keys * HEAD_DIM,
            bytes_accessed=heads * keys * 4 * HEAD_DIM * 2,
            transcendentals=len(qs) * heads * rows * keys,
        ),
        name=name,
    )(*qs, *[array for array, _, _ in gots], *[p for p, _ in pieces])


def after(value, *needed):
    return lax.optimization_barrier((value, *needed))[0]


def per_device(query_rows, key_rows, value_rows, query_tan, key_tan, value_tan):
    offs = jnp.stack(offsets()).astype(jnp.int32)
    own, to_one, to_two, to_three, own_q, to_two_q, to_three_q = pack(
        (key_rows, value_rows, key_tan, value_tan, query_rows, query_tan)
    )
    around = lambda array: [lax.ppermute(array, "x", perm) for perm in AROUND_X]
    swap = lambda arrays: [lax.ppermute(a, "core", SWAP) for a in arrays]
    one = lax.ppermute(to_one, Z, TO[0])
    two_q = lax.ppermute(to_two_q, Z, TO[1])
    own_x = around(own)
    one, two_q, own, own_x, to_two, to_three_q, to_three = lax.optimization_barrier(
        (one, two_q, own, own_x, to_two, to_three_q, to_three)
    )
    one, one_q = one[:KV_BLOCKS], one[KV_BLOCKS:]
    two = lax.ppermute(to_two, Z, TO[1])
    three_q = lax.ppermute(to_three_q, Z, TO[2])
    one_x = around(one)
    two, three_q, one, one_x, own, own_x, to_three = lax.optimization_barrier(
        (two, three_q, one, one_x, own, own_x, to_three)
    )
    three_ = lax.ppermute(to_three, Z, TO[2])
    two_x = around(two)
    own_s = lax.ppermute(jnp.concatenate([own, *own_x]), "core", SWAP)
    near_q = jnp.stack([own_q, one_q, two_q, three_q])
    three_, two, two_x, one, one_x, own_s, near_q = lax.optimization_barrier(
        (three_, two, two_x, one, one_x, own_s, near_q)
    )
    three_x = around(three_)
    far_q = lax.ppermute(near_q, Z, PAIR)
    both_s = lax.ppermute(jnp.concatenate([one, *one_x, two, *two_x, three_]), "core", SWAP)
    pieces = [(p, 0) for p in (own, *own_x, one, *one_x, two, *two_x)]
    pieces += [(own_s, i) for i in range(4)] + [(both_s, i) for i in range(8)]
    early = attend("early", [near_q], pieces, (0, HEADS_HERE))
    three_, three_x, far_q, early = lax.optimization_barrier((three_, three_x, far_q, early))
    three_s = swap(three_x)
    late = [(p, 0) for p in (three_, *three_x, *three_s)] + [(both_s, 8)]
    early_far = attend("early_far", [far_q], pieces, CHUNKS[0])
    paired, result, last, back = {}, (), (), []
    for kind, c in ORDER:
        chunk = CHUNKS[c]
        if kind == "far":
            if c == 0:
                part = attend(kind, [far_q], late, chunk, [(early_far, chunk[0], 0)])
            else:
                part = attend(kind, [after(far_q, *last)], pieces + late, chunk)
            paired[c] = lax.ppermute(after(part, *paired.values()), Z, PAIR)
            last = (part,)
        else:
            gots = [(early, 0, 0), (paired[c], chunk[0], 0)]
            near = attend(kind, [after(near_q, *last)], late, chunk, gots, last=True)
            if back:
                result = unpack(c - 1, offs, [after(back[0], *near), *back[1:]], result)
            back = [near[0]]
            back += [lax.ppermute(after(o, *result), Z, perm) for o, perm in zip(near[1:], BACK)]
            last = (near[0],)
    return tuple(unpack(len(CHUNKS) - 1, offs, back, result))


def solution(mesh):
    fine = Mesh(mesh.devices.reshape(4, 2, 4, 2, 4), AXES)
    rows = P(AXES, None)
    return jax.shard_map(
        per_device,
        mesh=fine,
        in_specs=(rows,) * 6,
        out_specs=(rows, rows),
        check_vma=False,
    )
```
